1024 devices in a mesh: section: 8 (over y_hi, core), tensor: 128 (over y_lo, x, z).
Axes of the slice: x: 8, y: 8 (y_hi: 4, y_lo: 2; y = y_hi * 2 + y_lo), z: 8, core: 2. Of those that a mesh axis runs over, the one named last changes fastest.
Arguments:
- acts: bfloat16 [8, 512, 4096], P('section', 'tensor'), may hold values from -6 to 6
- norm_gain: float32 [8, 4096], P('section'), may hold values from 0.1 to 1.9
- gate_w: bfloat16 [8, 128, 1024, 512], P('section', 'tensor'), may hold values from -0.09375 to 0.09375
- up_w: bfloat16 [8, 128, 1024, 512], P('section', 'tensor'), may hold values from -0.09375 to 0.09375
- down_w: bfloat16 [8, 128, 512, 1024], P('section', 'tensor'), may hold values from -0.046875 to 0.046875
Outputs:
- received: bfloat16 [8, 512, 4096], P('section', 'tensor')
The draws below stay inside these ranges and needn't reach their ends.
All inputs are finite; a program needn't handle non-finite values.
Results may differ from the reference program's by a relative error of at most 0.0051.
Values may be sent and summed in bfloat16 or wider, within the bound.
No kernel may reach another device: no remote copies, remote signals or barrier semaphores. Data moves between devices by JAX's collectives and lax.ppermute only.
A program may use at most 32 MiB of HBM per device.

```python
import jax
import jax.numpy as jnp
from jax import lax

D = 4096
FF = 16384
DGRP = 4
TOKENS = 512
DA = 1024
FB = 512
N_SECTION = 8
N_TENSOR = 128


def level_of(rng, shape, cuts, smallest, top_value):
    gain = 1.0
    for position, shards_of in cuts:
        steps = jax.random.uniform(jax.random.fold_in(jax.random.fold_in(rng, 6), position), (shards_of,), jnp.float32, smallest / len(cuts), top_value / len(cuts))
        gain = gain * jnp.repeat(jnp.exp(steps), shape[position] // shards_of).reshape((-1,) + (1,) * (len(shape) - 1 - position))
    return gain


def gaussian(rng, extent, scale, most, shards=(), held_as=jnp.bfloat16):
    values = scale * jax.random.normal(rng, extent, jnp.float32)
    if shards:
        values = values * level_of(rng, extent, shards, -0.22, 0.18)
    return jnp.clip(values, -most, most).astype(held_as)


def setup_inputs(seed: int = 0) -> dict:
    seeds = jax.random.split(jax.random.key(seed), 6)
    return {
        "acts": gaussian(seeds[0], (N_SECTION, TOKENS, D), 1.0, 6.0, ((0, 8), (1, 128))),
        "norm_gain": jnp.clip(1.0 + 0.18 * jax.random.normal(seeds[1], (N_SECTION, D), jnp.float32), 0.1, 1.9),
        "gate_w": gaussian(seeds[2], (N_SECTION, N_TENSOR, DA, FB), D ** -0.5, 0.09375, ((0, 8), (1, 128))),
        "up_w": gaussian(seeds[3], (N_SECTION, N_TENSOR, DA, FB), D ** -0.5, 0.09375, ((0, 8), (1, 128))),
        "down_w": gaussian(seeds[4], (N_SECTION, N_TENSOR, FB, DA), FF ** -0.5, 0.046875, ((0, 8), (1, 128))),
    }


def expand_input_side(blocks):
    groups = N_TENSOR // DGRP
    return blocks.reshape(groups, DGRP, DA, FB).transpose(1, 2, 0, 3).reshape(D, FF)

def expand_output_side(blocks):
    groups = N_TENSOR // DGRP
    return blocks.reshape(groups, DGRP, FB, DA).transpose(0, 2, 1, 3).reshape(FF, D)

def reference(acts, norm_gain, gate_w, up_w, down_w):
    blocks = []
    for section_index in range(N_SECTION):
        inputs = acts[section_index].astype(jnp.float32)
        scale = lax.rsqrt(lax.optimization_barrier(jnp.mean(inputs * inputs, axis=-1, keepdims=True)) + 1e-05)
        normed = (inputs * scale * norm_gain[section_index][None, :]).astype(jnp.bfloat16)
        gate = jnp.dot(normed, expand_input_side(gate_w[section_index]), preferred_element_type=jnp.float32)
        up_part = jnp.dot(normed, expand_input_side(up_w[section_index]), preferred_element_type=jnp.float32)
        hidden = (jax.nn.silu(gate) * up_part).astype(jnp.bfloat16)
        summed = jnp.dot(hidden, expand_output_side(down_w[section_index]), preferred_element_type=jnp.float32)
        blocks.append((inputs + summed).astype(jnp.bfloat16))
    first = jnp.zeros_like(blocks[0])[None]
    return jnp.concatenate([first, jnp.stack(blocks[:-1])], axis=0)
```

```python
import jax
import jax.numpy as jnp
from jax import lax
from jax.sharding import PartitionSpec as P


def quads(groups_a):
    count = lax.axis_size("tensor")
    return [list(range(low, low + groups_a)) for low in range(0, count, groups_a)]


def passed_along(value, axis, steps):
    count = lax.axis_size(axis)
    first, last = (max(0, -steps), min(count, count - steps))
    return lax.ppermute(value, axis, [(source, source + steps) for source in range(first, last)])


def per_device(acts, norm_gain, gate_w, up_w, down_w):
    inputs = acts[0].astype(jnp.float32)
    tokens, features = inputs.shape
    scale = lax.rsqrt(jnp.mean(inputs * inputs, axis=-1, keepdims=True) + 1e-05)
    normed = (inputs * scale * norm_gain[0][None, :]).astype(jnp.bfloat16)
    gate_local = gate_w[0, 0]
    up_local = up_w[0, 0]
    down_local = down_w[0, 0]
    depth, width = gate_local.shape
    devices = lax.axis_size("tensor")
    groups_a = features // depth
    groups_b = devices // groups_a
    total = devices * tokens

    by_block = jnp.transpose(normed.reshape(tokens, groups_a, depth), (1, 0, 2))
    sent = jnp.tile(by_block, (groups_b, 1, 1))
    columns = lax.all_to_all(sent, "tensor", 0, 0, tiled=True).reshape(total, depth)

    gate = jnp.dot(columns, gate_local, preferred_element_type=jnp.float32)
    up_part = jnp.dot(columns, up_local, preferred_element_type=jnp.float32)
    both = jnp.concatenate([gate.astype(jnp.bfloat16), up_part.astype(jnp.bfloat16)], axis=1)
    shares = both.reshape(groups_a, total // groups_a, 2 * width)
    shares = lax.all_to_all(shares, "tensor", 0, 0, axis_index_groups=quads(groups_a), tiled=True)
    summed = jnp.sum(shares.astype(jnp.float32), axis=0)
    hidden = (jax.nn.silu(summed[:, :width]) * summed[:, width:]).astype(jnp.bfloat16)
    hidden = jnp.tile(hidden[None], (groups_a, 1, 1))
    hidden = lax.all_to_all(hidden, "tensor", 0, 0, axis_index_groups=quads(groups_a), tiled=True)
    hidden = hidden.reshape(total, width)

    partial_rows = jnp.dot(hidden, down_local, preferred_element_type=jnp.float32)
    sent = partial_rows.astype(jnp.bfloat16).reshape(devices, tokens, depth)
    parts = lax.all_to_all(sent, "tensor", 0, 0, tiled=True)
    parts = parts.reshape(groups_b, groups_a, tokens, depth).astype(jnp.float32)
    rows = jnp.transpose(jnp.sum(parts, axis=0), (1, 0, 2)).reshape(tokens, features)
    block = (inputs + rows).astype(jnp.bfloat16)
    return passed_along(block, "section", 1)[None]


def solution(mesh):
    in_specs = (
        P("section", "tensor", None),
        P("section", None),
        P("section", "tensor", None, None),
        P("section", "tensor", None, None),
        P("section", "tensor", None, None),
    )
    out_specs = P("section", "tensor", None)
    return jax.shard_map(
        per_device, mesh=mesh, in_specs=in_specs, out_specs=out_specs, check_vma=False
    )
```

```python
import jax
import jax.numpy as jnp
from jax import lax
from jax.sharding import PartitionSpec as P


def runs(size):
    count = lax.axis_size("tensor")
    return [list(range(low, low + size)) for low in range(0, count, size)]


def traded(blocks, size):
    return lax.all_to_all(blocks, "tensor", 0, 0, axis_index_groups=runs(size), tiled=True)


def mirrored(values):
    count = lax.axis_size("tensor")
    half = count // 2
    return lax.ppermute(values, "tensor", [(i, (i + half) % count) for i in range(count)])


def passed_along(value, axis, steps):
    count = lax.axis_size(axis)
    first, last = (max(0, -steps), min(count, count - steps))
    return lax.ppermute(value, axis, [(source, source + steps) for source in range(first, last)])


def per_device(acts, norm_gain, gate_w, up_w, down_w):
    inputs = acts[0].astype(jnp.float32)
    tokens, features = inputs.shape
    scale = lax.rsqrt(jnp.mean(inputs * inputs, axis=-1, keepdims=True) + 1e-05)
    normed = (inputs * scale * norm_gain[0][None, :]).astype(jnp.bfloat16)
    gate_local = gate_w[0, 0]
    up_local = up_w[0, 0]
    down_local = down_w[0, 0]
    depth, width = gate_local.shape
    groups_a = features // depth
    near = lax.axis_size("tensor") // 2
    groups_b = near // groups_a
    total = near * tokens

    def hidden_share(columns):
        gate = jnp.dot(columns, gate_local, preferred_element_type=jnp.float32)
        up_part = jnp.dot(columns, up_local, preferred_element_type=jnp.float32)
        both = jnp.concatenate([gate.astype(jnp.bfloat16), up_part.astype(jnp.bfloat16)], axis=1)
        shares = traded(both.reshape(groups_a, total // groups_a, 2 * width), groups_a)
        summed = jnp.sum(shares.astype(jnp.float32), axis=0)
        return (jax.nn.silu(summed[:, :width]) * summed[:, width:]).astype(jnp.bfloat16)

    def down_rows(share):
        hidden = traded(jnp.tile(share[None], (groups_a, 1, 1)), groups_a).reshape(total, width)
        return jnp.dot(hidden, down_local, preferred_element_type=jnp.float32)

    by_block = jnp.transpose(normed.reshape(tokens, groups_a, depth), (1, 0, 2))
    near_columns = traded(jnp.tile(by_block, (groups_b, 1, 1)), near).reshape(total, depth)
    far_columns = mirrored(near_columns)
    near_share = hidden_share(near_columns)
    far_share = hidden_share(far_columns)

    far_rows = mirrored(down_rows(far_share).astype(jnp.bfloat16))
    rows = down_rows(near_share) + far_rows.astype(jnp.float32)
    parts = traded(rows.astype(jnp.bfloat16).reshape(near, tokens, depth), near)
    parts = parts.reshape(groups_b, groups_a, tokens, depth).astype(jnp.float32)
    summed = jnp.transpose(jnp.sum(parts, axis=0), (1, 0, 2)).reshape(tokens, features)
    block = (inputs + summed).astype(jnp.bfloat16)
    return passed_along(block, "section", 1)[None]


def solution(mesh):
    in_specs = (
        P("section", "tensor", None),
        P("section", None),
        P("section", "tensor", None, None),
        P("section", "tensor", None, None),
        P("section", "tensor", None, None),
    )
    out_specs = P("section", "tensor", None)
    return jax.shard_map(
        per_device, mesh=mesh, in_specs=in_specs, out_specs=out_specs, check_vma=False
    )
```

```python
import jax
import jax.numpy as jnp
from jax import lax
from jax.experimental import pallas as pl
from jax.experimental.pallas import tpu as pltpu
from jax.sharding import PartitionSpec as P

f32, bf16 = jnp.float32, jnp.bfloat16


def runs(size):
    count = lax.axis_size("tensor")
    return [list(range(low, low + size)) for low in range(0, count, size)]


def traded(blocks, size):
    return lax.all_to_all(blocks, "tensor", 0, 0, axis_index_groups=runs(size), tiled=True)


def mirrored(values):
    count = lax.axis_size("tensor")
    half = count // 2
    return lax.ppermute(values, "tensor", [(i, (i + half) % count) for i in range(count)])


def passed_along(value, axis, steps):
    count = lax.axis_size(axis)
    first, last = (max(0, -steps), min(count, count - steps))
    return lax.ppermute(value, axis, [(source, source + steps) for source in range(first, last)])


def dot(left, right):
    return jnp.dot(left, right, preferred_element_type=f32)


def local(body, outs, flops, moved, *operands):
    spec = pl.BlockSpec(memory_space=pltpu.VMEM)
    return pl.pallas_call(
        body,
        out_shape=[jax.ShapeDtypeStruct(shape, bf16) for shape in outs],
        in_specs=[spec] * len(operands),
        out_specs=[spec] * len(outs),
        compiler_params=pltpu.CompilerParams(vmem_limit_bytes=24 * 2**20),
        cost_estimate=pl.CostEstimate(flops=flops, bytes_accessed=moved, transcendentals=0),
    )(*operands)


def norm_kernel(acts_ref, gain_ref, out_ref):
    count, _, depth = out_ref.shape
    inputs = acts_ref[...].astype(f32)
    groups = inputs.shape[1] // depth
    scale = lax.rsqrt(jnp.mean(inputs * inputs, axis=-1, keepdims=True) + 1e-05)
    normed = (inputs * scale * gain_ref[...]).astype(bf16)
    for block in range(count):
        low = block % groups * depth
        out_ref[block] = normed[:, low : low + depth]


def gate_up(columns_ref, gate_ref, up_ref, both_ref):
    width = gate_ref.shape[1]
    both_ref[:, :width] = dot(columns_ref[...], gate_ref[...]).astype(bf16)
    both_ref[:, width:] = dot(columns_ref[...], up_ref[...]).astype(bf16)


def gated(shares_ref):
    width = shares_ref.shape[2] // 2
    total = shares_ref[0].astype(f32)
    for part in range(1, shares_ref.shape[0]):
        total = total + shares_ref[part].astype(f32)
    gate = total[:, :width]
    return (gate / (1.0 + jnp.exp(-gate)) * total[:, width:]).astype(bf16)


def gate_up_and_gated(shares_ref, columns_ref, gate_ref, up_ref, both_ref, share_ref):
    gate_up(columns_ref, gate_ref, up_ref, both_ref)
    share_ref[...] = gated(shares_ref)


def copies(share, out_ref):
    for block in range(out_ref.shape[0]):
        out_ref[block] = share


def gated_copies(shares_ref, out_ref):
    copies(gated(shares_ref), out_ref)


def down_far(hidden_ref, down_ref, share_ref, rows_ref, out_ref):
    rows_ref[...] = dot(hidden_ref[...], down_ref[...]).astype(bf16)
    copies(share_ref[...], out_ref)


def down_near(hidden_ref, down_ref, far_ref, rows_ref):
    own = dot(hidden_ref[...], down_ref[...])
    rows_ref[...] = (own + far_ref[...].astype(f32)).astype(bf16)


def per_device(acts, norm_gain, gate_w, up_w, down_w):
    gate_local, up_local, down_local = gate_w[0, 0], up_w[0, 0], down_w[0, 0]
    tokens, features = acts.shape[1:]
    depth, width = gate_local.shape
    groups_a = features // depth
    near = lax.axis_size("tensor") // 2
    groups_b = near // groups_a
    total = near * tokens
    piece = total // groups_a
    cost = 2 * total * depth * width
    weight = 2 * depth * width

    (sent,) = local(norm_kernel, [(near, tokens, depth)], 0, 2 * total * depth, acts[0], norm_gain)
    near_columns = traded(sent, near).reshape(total, depth)
    far_columns = mirrored(near_columns)

    (both,) = local(
        gate_up, [(total, 2 * width)], 2 * cost, 2 * weight, near_columns, gate_local, up_local
    )
    shares = traded(both.reshape(groups_a, piece, 2 * width), groups_a)
    both, near_share = local(
        gate_up_and_gated,
        [(total, 2 * width), (piece, width)],
        2 * cost,
        2 * weight,
        shares,
        far_columns,
        gate_local,
        up_local,
    )
    shares = traded(both.reshape(groups_a, piece, 2 * width), groups_a)
    (spread,) = local(gated_copies, [(groups_a, piece, width)], 0, 2 * total * width, shares)
    hidden = traded(spread, groups_a).reshape(total, width)
    far_rows, spread = local(
        down_far,
        [(total, depth), (groups_a, piece, width)],
        cost,
        weight,
        hidden,
        down_local,
        near_share,
    )
    far_rows = mirrored(far_rows)
    hidden = traded(spread, groups_a).reshape(total, width)
    (rows,) = local(down_near, [(total, depth)], cost, weight, hidden, down_local, far_rows)

    parts = traded(rows.reshape(near, tokens, depth), near)
    parts = parts.reshape(groups_b, groups_a, tokens, depth).astype(f32)
    summed = jnp.transpose(jnp.sum(parts, axis=0), (1, 0, 2)).reshape(tokens, features)
    block = (acts[0].astype(f32) + summed).astype(bf16)
    return passed_along(block, "section", 1)[None]


def solution(mesh):
    in_specs = (
        P("section", "tensor", None),
        P("section", None),
        P("section", "tensor", None, None),
        P("section", "tensor", None, None),
        P("section", "tensor", None, None),
    )
    out_specs = P("section", "tensor", None)
    return jax.shard_map(
        per_device, mesh=mesh, in_specs=in_specs, out_specs=out_specs, check_vma=False
    )
```

```python
import jax
import jax.numpy as jnp
from jax import lax
from jax.experimental import pallas as pl
from jax.experimental.pallas import tpu as pltpu
from jax.sharding import PartitionSpec as P

f32, bf16 = jnp.float32, jnp.bfloat16


def runs(size):
    count = lax.axis_size("tensor")
    return [list(range(low, low + size)) for low in range(0, count, size)]


def traded(blocks, size):
    return lax.all_to_all(blocks, "tensor", 0, 0, axis_index_groups=runs(size), tiled=True)


def flipped(values, mask):
    count = lax.axis_size("tensor")
    return lax.ppermute(values, "tensor", [(i, i ^ mask) for i in range(count)])


def passed_along(value, mask):
    sections, count = lax.axis_size("section"), lax.axis_size("tensor")
    route = [
        (section * count + place, (section + 1) * count + (place ^ mask))
        for section in range(sections - 1)
        for place in range(count)
    ]
    return lax.ppermute(value, ("section", "tensor"), route)


def dot(left, right):
    return jnp.dot(left, right, preferred_element_type=f32)


def local(body, outs, flops, moved, *operands, scratch=(), after=()):
    spec = pl.BlockSpec(memory_space=pltpu.VMEM)

    def kernel(*refs):
        body(*refs[len(after) :])

    return pl.pallas_call(
        kernel,
        out_shape=[jax.ShapeDtypeStruct(shape, kind) for shape, kind in outs],
        in_specs=[pl.BlockSpec(memory_space=pl.ANY)] * len(after) + [spec] * len(operands),
        out_specs=[spec] * len(outs),
        scratch_shapes=[pltpu.VMEM(shape, kind) for shape, kind in scratch],
        compiler_params=pltpu.CompilerParams(vmem_limit_bytes=24 * 2**20),
        cost_estimate=pl.CostEstimate(flops=flops, bytes_accessed=moved, transcendentals=0),
    )(*after, *operands)


def norm_kernel(acts_ref, gain_ref, out_ref):
    count, _, depth = out_ref.shape
    inputs = acts_ref[...].astype(f32)
    groups = inputs.shape[1] // depth
    scale = lax.rsqrt(jnp.mean(inputs * inputs, axis=-1, keepdims=True) + 1e-05)
    normed = (inputs * scale * gain_ref[...]).astype(bf16)
    for block in range(count):
        low = block % groups * depth
        out_ref[block] = normed[:, low : low + depth]


def rows_of(step, groups, piece):
    member = lax.rem(lax.axis_index("tensor"), groups) ^ step
    return pl.ds(pl.multiple_of(member * piece, piece), piece)


def gate_up_kernel(columns_ref, gate_ref, up_ref, own_ref, *rest):
    *sent_refs, sums_ref = rest
    width = gate_ref.shape[1]
    piece, groups = own_ref.shape[0], len(sent_refs) + 1
    sums_ref[:, :width] = dot(columns_ref[...], gate_ref[...])
    sums_ref[:, width:] = dot(columns_ref[...], up_ref[...])
    own_ref[...] = sums_ref[rows_of(0, groups, piece)]
    for step in range(1, groups):
        sent_refs[step - 1][...] = sums_ref[rows_of(step, groups, piece)].astype(bf16)


def gated_kernel(own_ref, *rest):
    *got_refs, share_ref = rest
    width = share_ref.shape[1]
    total = own_ref[...]
    for got_ref in got_refs:
        total = total + got_ref[...].astype(f32)
    gate = total[:, :width]
    share_ref[...] = (gate / (1.0 + jnp.exp(-gate)) * total[:, width:]).astype(bf16)


def gathered(share_refs, hidden_ref):
    piece, groups = share_refs[0].shape[0], len(share_refs)
    for step in range(groups):
        hidden_ref[rows_of(step, groups, piece)] = share_refs[step][...]
    return hidden_ref[...]


def down_kernel(down_ref, *rest):
    *share_refs, rows_ref, hidden_ref = rest
    rows_ref[...] = dot(gathered(share_refs, hidden_ref), down_ref[...]).astype(bf16)


def down_add_kernel(down_ref, other_ref, *rest):
    *share_refs, rows_ref, hidden_ref = rest
    own = dot(gathered(share_refs, hidden_ref), down_ref[...])
    rows_ref[...] = (own + other_ref[...].astype(f32)).astype(bf16)


def per_device(acts, norm_gain, gate_w, up_w, down_w):
    gate_local, up_local, down_local = gate_w[0, 0], up_w[0, 0], down_w[0, 0]
    tokens, features = acts.shape[1:]
    depth, width = gate_local.shape
    groups_a = features // depth
    near = lax.axis_size("tensor") // 2
    groups_b = near // groups_a
    total = near * tokens
    piece = total // groups_a
    cost = 2 * total * depth * width
    weight = 2 * depth * width

    def partial_sums(columns):
        own, *sent = local(
            gate_up_kernel,
            [((piece, 2 * width), f32)] + [((piece, 2 * width), bf16)] * (groups_a - 1),
            2 * cost,
            2 * weight,
            columns,
            gate_local,
            up_local,
            scratch=[((total, 2 * width), f32)],
        )
        return [own] + [flipped(part, step + 1) for step, part in enumerate(sent)]

    def hidden_shares(parts, after=()):
        shape = (piece, width)
        (share,) = local(gated_kernel, [(shape, bf16)], 0, 2 * total * width, *parts, after=after)
        return [share] + [flipped(share, step) for step in range(1, groups_a)]

    def down(kernel, *operands, after=()):
        (rows,) = local(
            kernel,
            [((total, depth), bf16)],
            cost,
            weight,
            down_local,
            *operands,
            scratch=[((total, width), bf16)],
            after=after,
        )
        return rows

    mirror_acts = flipped(acts[0], near)
    (sent,) = local(
        norm_kernel, [((near, tokens, depth), bf16)], 0, 2 * total * depth, acts[0], norm_gain
    )
    near_columns = traded(sent, near).reshape(total, depth)
    far_columns = flipped(near_columns, near)
    near_parts = partial_sums(near_columns)
    far_parts = partial_sums(far_columns)
    near_hidden = hidden_shares(near_parts, after=far_parts[:1])
    far_hidden = hidden_shares(far_parts)

    mirror_rows = flipped(down(down_kernel, *near_hidden, after=far_parts[1:]), near)
    rows = down(down_add_kernel, mirror_rows, *far_hidden)
    parts = traded(rows.reshape(near, tokens, depth), near)
    parts = parts.reshape(groups_b, groups_a, tokens, depth).astype(f32)
    summed = jnp.transpose(jnp.sum(parts, axis=0), (1, 0, 2)).reshape(tokens, features)
    block = (mirror_acts.astype(f32) + summed).astype(bf16)
    return passed_along(block, near)[None]


def solution(mesh):
    in_specs = (
        P("section", "tensor", None),
        P("section", None),
        P("section", "tensor", None, None),
        P("section", "tensor", None, None),
        P("section", "tensor", None, None),
    )
    out_specs = P("section", "tensor", None)
    return jax.shard_map(
        per_device, mesh=mesh, in_specs=in_specs, out_specs=out_specs, check_vma=False
    )
```

```python
import jax
import jax.numpy as jnp
from jax import lax
from jax.experimental import pallas as pl
from jax.experimental.pallas import tpu as pltpu
from jax.sharding import PartitionSpec as P

f32, bf16 = jnp.float32, jnp.bfloat16


def runs(size):
    count = lax.axis_size("tensor")
    return [list(range(low, low + size)) for low in range(0, count, size)]


def traded(blocks, size):
    return lax.all_to_all(blocks, "tensor", 0, 0, axis_index_groups=runs(size), tiled=True)


def flipped(values, mask):
    count = lax.axis_size("tensor")
    return lax.ppermute(values, "tensor", [(i, i ^ mask) for i in range(count)])


def passed_along(value, mask):
    sections, count = lax.axis_size("section"), lax.axis_size("tensor")
    route = [
        (section * count + place, (section + 1) * count + (place ^ mask))
        for section in range(sections - 1)
        for place in range(count)
    ]
    return lax.ppermute(value, ("section", "tensor"), route)


def dot(left, right):
    return jnp.dot(left, right, preferred_element_type=f32)


def local(body, outs, flops, moved, *operands):
    spec = pl.BlockSpec(memory_space=pltpu.VMEM)
    return pl.pallas_call(
        body,
        out_shape=[jax.ShapeDtypeStruct(shape, bf16) for shape in outs],
        in_specs=[spec] * len(operands),
        out_specs=[spec] * len(outs),
        compiler_params=pltpu.CompilerParams(vmem_limit_bytes=24 * 2**20),
        cost_estimate=pl.CostEstimate(flops=flops, bytes_accessed=moved, transcendentals=0),
    )(*operands)


def norm_kernel(acts_ref, gain_ref, out_ref):
    count, _, depth = out_ref.shape
    inputs = acts_ref[...].astype(f32)
    groups = inputs.shape[1] // depth
    scale = lax.rsqrt(jnp.mean(inputs * inputs, axis=-1, keepdims=True) + 1e-05)
    normed = (inputs * scale * gain_ref[...]).astype(bf16)
    for block in range(count):
        low = block % groups * depth
        out_ref[block] = normed[:, low : low + depth]


def gate_up(columns_ref, gate_ref, up_ref, out_ref):
    width = gate_ref.shape[1]
    out_ref[:, :width] = dot(columns_ref[...], gate_ref[...]).astype(bf16)
    out_ref[:, width : 2 * width] = dot(columns_ref[...], up_ref[...]).astype(bf16)


def gated(shares_ref, width):
    total = shares_ref[0, :, : 2 * width].astype(f32)
    for part in range(1, shares_ref.shape[0]):
        total = total + shares_ref[part, :, : 2 * width].astype(f32)
    gate = total[:, :width]
    return (gate / (1.0 + jnp.exp(-gate)) * total[:, width:]).astype(bf16)


def near_share_kernel(shares_ref, share_ref):
    share_ref[...] = gated(shares_ref, share_ref.shape[1])


def far_sums_near_share(columns_ref, share_ref, gate_ref, up_ref, out_ref):
    piece, width = share_ref.shape
    gate_up(columns_ref, gate_ref, up_ref, out_ref)
    for low in range(0, out_ref.shape[0], piece):
        out_ref[low : low + piece, 2 * width :] = share_ref[...]


def near_down_far_share(got_ref, down_ref, rows_ref, spread_ref):
    groups, piece, _ = got_ref.shape
    width = down_ref.shape[0]
    hidden = got_ref[:, :, 2 * width :].reshape(groups * piece, width)
    rows_ref[...] = dot(hidden, down_ref[...]).astype(bf16)
    share = gated(got_ref, width)
    for part in range(groups):
        spread_ref[part] = share


def far_down(hidden_ref, down_ref, other_ref, rows_ref):
    own = dot(hidden_ref[...], down_ref[...])
    rows_ref[...] = (own + other_ref[...].astype(f32)).astype(bf16)


def per_device(acts, norm_gain, gate_w, up_w, down_w):
    gate_local, up_local, down_local = gate_w[0, 0], up_w[0, 0], down_w[0, 0]
    tokens, features = acts.shape[1:]
    depth, width = gate_local.shape
    groups_a = features // depth
    near = lax.axis_size("tensor") // 2
    groups_b = near // groups_a
    total = near * tokens
    piece = total // groups_a
    cost = 2 * total * depth * width
    weight = 2 * depth * width

    mirror_acts = flipped(acts[0], near)
    (sent,) = local(norm_kernel, [(near, tokens, depth)], 0, 2 * total * depth, acts[0], norm_gain)
    near_columns = traded(sent, near).reshape(total, depth)
    far_columns = flipped(near_columns, near)

    (sums,) = local(
        gate_up, [(total, 2 * width)], 2 * cost, 2 * weight, near_columns, gate_local, up_local
    )
    shares = traded(sums.reshape(groups_a, piece, 2 * width), groups_a)
    (near_share,) = local(near_share_kernel, [(piece, width)], 0, 2 * total * width, shares)
    (sums,) = local(
        far_sums_near_share,
        [(total, 3 * width)],
        2 * cost,
        2 * weight,
        far_columns,
        near_share,
        gate_local,
        up_local,
    )
    got = traded(sums.reshape(groups_a, piece, 3 * width), groups_a)
    near_rows, spread = local(
        near_down_far_share,
        [(total, depth), (groups_a, piece, width)],
        cost,
        weight,
        got,
        down_local,
    )

    mirror_rows = flipped(near_rows, near)
    hidden = traded(spread, groups_a).reshape(total, width)
    (rows,) = local(far_down, [(total, depth)], cost, weight, hidden, down_local, mirror_rows)
    parts = traded(rows.reshape(near, tokens, depth), near)
    parts = parts.reshape(groups_b, groups_a, tokens, depth).astype(f32)
    summed = jnp.transpose(jnp.sum(parts, axis=0), (1, 0, 2)).reshape(tokens, features)
    block = (mirror_acts.astype(f32) + summed).astype(bf16)
    return passed_along(block, near)[None]


def solution(mesh):
    in_specs = (
        P("section", "tensor", None),
        P("section", None),
        P("section", "tensor", None, None),
        P("section", "tensor", None, None),
        P("section", "tensor", None, None),
    )
    out_specs = P("section", "tensor", None)
    return jax.shard_map(
        per_device, mesh=mesh, in_specs=in_specs, out_specs=out_specs, check_vma=False
    )
```

```python
import jax
import jax.numpy as jnp
from jax import lax
from jax.experimental import pallas as pl
from jax.experimental.pallas import tpu as pltpu
from jax.sharding import PartitionSpec as P

f32, bf16 = jnp.float32, jnp.bfloat16


def runs(size):
    count = lax.axis_size("tensor")
    return [list(range(low, low + size)) for low in range(0, count, size)]


def every_other(run, size):
    count = lax.axis_size("tensor")
    return [
        [low + place for place in range(run) if place // size % 2 == half]
        for low in range(0, count, run)
        for half in range(2)
    ]


def traded(blocks, groups):
    return lax.all_to_all(blocks, "tensor", 0, 0, axis_index_groups=groups, tiled=True)


def flipped(values, mask):
    count = lax.axis_size("tensor")
    return lax.ppermute(values, "tensor", [(i, i ^ mask) for i in range(count)])


def passed_along(value, mask):
    sections, count = lax.axis_size("section"), lax.axis_size("tensor")
    route = [
        (section * count + place, (section + 1) * count + (place ^ mask))
        for section in range(sections - 1)
        for place in range(count)
    ]
    return lax.ppermute(value, ("section", "tensor"), route)


def dot(left, right):
    return jnp.dot(left, right, preferred_element_type=f32)


def local(body, outs, flops, moved, *operands):
    spec = pl.BlockSpec(memory_space=pltpu.VMEM)
    return pl.pallas_call(
        body,
        out_shape=[jax.ShapeDtypeStruct(shape, kind) for shape, kind in outs],
        in_specs=[spec] * len(operands),
        out_specs=[spec] * len(outs),
        compiler_params=pltpu.CompilerParams(vmem_limit_bytes=24 * 2**20),
        cost_estimate=pl.CostEstimate(flops=flops, bytes_accessed=moved, transcendentals=0),
    )(*operands)


def norm_kernel(acts_ref, gain_ref, out_ref, rows_ref):
    count, _, depth = out_ref.shape
    inputs = acts_ref[...].astype(f32)
    groups = inputs.shape[1] // depth
    blocks = [inputs[:, low : low + depth] for low in range(0, groups * depth, depth)]
    rows_ref[...] = jnp.concatenate(blocks, axis=0).astype(bf16)
    scale = lax.rsqrt(jnp.mean(inputs * inputs, axis=-1, keepdims=True) + 1e-05)
    normed = (inputs * scale * gain_ref[...]).astype(bf16)
    for block in range(count):
        low = block % groups * depth
        out_ref[block] = normed[:, low : low + depth]


def gate_up(columns_ref, gate_ref, up_ref, out_ref):
    total, width = out_ref.shape[0], gate_ref.shape[1]
    out_ref[:, :width] = dot(columns_ref[:total], gate_ref[...]).astype(bf16)
    out_ref[:, width : 2 * width] = dot(columns_ref[:total], up_ref[...]).astype(bf16)


def ordered_gate_up(got_ref, acts_ref, gate_ref, up_ref, columns_ref, out_ref):
    count, tokens, _ = got_ref.shape
    groups = acts_ref.shape[0] // tokens
    places = [
        low + member + half * groups
        for low in range(0, count, 2 * groups)
        for member in range(groups)
        for half in range(2)
    ]
    for start in range(0, count, 4):
        pieces = [got_ref[place].astype(f32) for place in places[start : start + 4]]
        rows = slice(start * tokens, (start + 4) * tokens)
        columns_ref[rows] = jnp.concatenate(pieces, axis=0).astype(bf16)
    columns_ref[count * tokens :] = acts_ref[...]
    gate_up(columns_ref, gate_ref, up_ref, out_ref)


def gated(shares_ref, width):
    total = shares_ref[0, :, : 2 * width].astype(f32)
    for part in range(1, shares_ref.shape[0]):
        total = total + shares_ref[part, :, : 2 * width].astype(f32)
    gate = total[:, :width]
    return (gate / (1.0 + jnp.exp(-gate)) * total[:, width:]).astype(bf16)


def near_share_kernel(shares_ref, share_ref):
    share_ref[...] = gated(shares_ref, share_ref.shape[1])


def far_sums_near_share(columns_ref, share_ref, gate_ref, up_ref, out_ref):
    piece, width = share_ref.shape
    gate_up(columns_ref, gate_ref, up_ref, out_ref)
    for low in range(0, out_ref.shape[0], piece):
        out_ref[low : low + piece, 2 * width :] = share_ref[...]


def near_down_far_share(got_ref, down_ref, rows_ref, spread_ref):
    groups, piece, _ = got_ref.shape
    width = down_ref.shape[0]
    hidden = got_ref[:, :, 2 * width :].reshape(groups * piece, width)
    rows_ref[...] = dot(hidden, down_ref[...]).astype(bf16)
    share = gated(got_ref, width)
    for part in range(groups):
        spread_ref[part] = share


def far_down(hidden_ref, down_ref, other_ref, rows_ref):
    own = dot(hidden_ref[...], down_ref[...])
    rows_ref[...] = (own + other_ref[...].astype(f32)).astype(bf16)


def finish(parts_ref, far_ref, own_ref, other_ref):
    tokens, features = own_ref.shape
    depth = parts_ref.shape[2]
    groups = features // depth
    upper = lax.axis_index("tensor") // groups % 2
    acts = far_ref[far_ref.shape[0] - tokens * groups :].astype(f32)
    for block in range(groups):
        total = parts_ref[block].astype(f32)
        for part in range(block + groups, parts_ref.shape[0], groups):
            total = total + parts_ref[part].astype(f32)
        low, high = total[:tokens], total[tokens:]
        columns = slice(block * depth, (block + 1) * depth)
        residual = acts[block * tokens : (block + 1) * tokens]
        own_ref[:, columns] = residual + jnp.where(upper == 0, low, high)
        other_ref[:, columns] = jnp.where(upper == 0, high, low)


def per_device(acts, norm_gain, gate_w, up_w, down_w):
    gate_local, up_local, down_local = gate_w[0, 0], up_w[0, 0], down_w[0, 0]
    tokens, features = acts.shape[1:]
    depth, width = gate_local.shape
    groups_a = features // depth
    near = lax.axis_size("tensor") // 2
    total = near * tokens
    piece = total // groups_a
    cost = 2 * total * depth * width
    weight = 2 * depth * width
    quads = runs(groups_a)

    sent, acts_rows = local(
        norm_kernel,
        [((near, tokens, depth), bf16), ((groups_a * tokens, depth), bf16)],
        0,
        2 * total * depth,
        acts[0],
        norm_gain,
    )
    near_columns, sums = local(
        ordered_gate_up,
        [((total + groups_a * tokens, depth), bf16), ((total, 2 * width), bf16)],
        2 * cost,
        2 * weight,
        traded(sent, runs(near)),
        acts_rows,
        gate_local,
        up_local,
    )
    far_columns = flipped(near_columns, near)
    shares = traded(sums.reshape(groups_a, piece, 2 * width), quads)
    (near_share,) = local(
        near_share_kernel, [((piece, width), bf16)], 0, 2 * total * width, shares
    )
    (sums,) = local(
        far_sums_near_share,
        [((total, 3 * width), bf16)],
        2 * cost,
        2 * weight,
        far_columns,
        near_share,
        gate_local,
        up_local,
    )
    got = traded(sums.reshape(groups_a, piece, 3 * width), quads)
    near_rows, spread = local(
        near_down_far_share,
        [((total, depth), bf16), ((groups_a, piece, width), bf16)],
        cost,
        weight,
        got,
        down_local,
    )

    mirror_rows = flipped(near_rows, near)
    hidden = traded(spread, quads).reshape(total, width)
    (rows,) = local(
        far_down, [((total, depth), bf16)], cost, weight, hidden, down_local, mirror_rows
    )
    rows = rows.reshape(near // 2, 2 * tokens, depth)
    parts = traded(rows, every_other(near, groups_a))
    own, other = local(
        finish, [((tokens, features), f32)] * 2, 0, 2 * total * depth, parts, far_columns
    )
    block = passed_along(own, near) + passed_along(other, near ^ groups_a)
    return block.astype(bf16)[None]


def solution(mesh):
    in_specs = (
        P("section", "tensor", None),
        P("section", None),
        P("section", "tensor", None, None),
        P("section", "tensor", None, None),
        P("section", "tensor", None, None),
    )
    out_specs = P("section", "tensor", None)
    return jax.shard_map(
        per_device, mesh=mesh, in_specs=in_specs, out_specs=out_specs, check_vma=False
    )
```

```python
import jax
import jax.numpy as jnp
from jax import lax
from jax.experimental import pallas as pl
from jax.experimental.pallas import tpu as pltpu
from jax.sharding import PartitionSpec as P

f32, bf16 = jnp.float32, jnp.bfloat16


def runs(size):
    count = lax.axis_size("tensor")
    return [list(range(low, low + size)) for low in range(0, count, size)]


def traded(blocks, size):
    return lax.all_to_all(blocks, "tensor", 0, 0, axis_index_groups=runs(size), tiled=True)


def flipped(values, mask):
    count = lax.axis_size("tensor")
    return lax.ppermute(values, "tensor", [(i, i ^ mask) for i in range(count)])


def passed_along(value, mask):
    sections, count = lax.axis_size("section"), lax.axis_size("tensor")
    route = [
        (section * count + place, (section + 1) * count + (place ^ mask))
        for section in range(sections - 1)
        for place in range(count)
    ]
    return lax.ppermute(value, ("section", "tensor"), route)


def dot(left, right):
    return jnp.dot(left, right, preferred_element_type=f32)


def local(body, outs, flops, moved, *operands, after=(), scratch=(), fetches=False):
    spec = pl.BlockSpec(memory_space=pl.ANY if fetches else pltpu.VMEM)
    limit = (56 if fetches else 24) * 2**20

    def kernel(*refs):
        body(*refs[len(after) :])

    return pl.pallas_call(
        kernel,
        out_shape=[jax.ShapeDtypeStruct(shape, bf16) for shape in outs],
        in_specs=[pl.BlockSpec(memory_space=pl.ANY)] * len(after) + [spec] * len(operands),
        out_specs=[pl.BlockSpec(memory_space=pltpu.VMEM)] * len(outs),
        scratch_shapes=scratch,
        compiler_params=pltpu.CompilerParams(vmem_limit_bytes=limit),
        cost_estimate=pl.CostEstimate(flops=flops, bytes_accessed=moved, transcendentals=0),
    )(*after, *operands)


def norm_kernel(acts_hbm, gain_hbm, out_ref, acts_ref, gain_ref, acts_sem, gain_sem):
    acts_copy = pltpu.make_async_copy(acts_hbm, acts_ref, acts_sem)
    gain_copy = pltpu.make_async_copy(gain_hbm, gain_ref, gain_sem)
    acts_copy.start()
    gain_copy.start()
    count, _, depth = out_ref.shape
    acts_copy.wait()
    gain_copy.wait()
    inputs = acts_ref[0].astype(f32)
    groups = inputs.shape[1] // depth
    scale = lax.rsqrt(jnp.mean(inputs * inputs, axis=-1, keepdims=True) + 1e-05)
    normed = (inputs * scale * gain_ref[...]).astype(bf16)
    for block in range(count):
        low = block % groups * depth
        out_ref[block] = normed[:, low : low + depth]


def gate_up(columns_ref, gate_ref, up_ref, out_ref):
    width = gate_ref.shape[1]
    out_ref[:, :width] = dot(columns_ref[...], gate_ref[...]).astype(bf16)
    out_ref[:, width : 2 * width] = dot(columns_ref[...], up_ref[...]).astype(bf16)


def gated(shares_ref, width):
    total = shares_ref[0, :, : 2 * width].astype(f32)
    for part in range(1, shares_ref.shape[0]):
        total = total + shares_ref[part, :, : 2 * width].astype(f32)
    gate = total[:, :width]
    return (gate / (1.0 + jnp.exp(-gate)) * total[:, width:]).astype(bf16)


def near_share_kernel(shares_ref, share_ref):
    share_ref[...] = gated(shares_ref, share_ref.shape[1])


def far_sums_near_share(columns_ref, share_ref, gate_ref, up_ref, out_ref):
    piece, width = share_ref.shape
    gate_up(columns_ref, gate_ref, up_ref, out_ref)
    for low in range(0, out_ref.shape[0], piece):
        out_ref[low : low + piece, 2 * width :] = share_ref[...]


def near_down_far_share(got_ref, down_ref, rows_ref, spread_ref):
    groups, piece, _ = got_ref.shape
    width = down_ref.shape[0]
    hidden = got_ref[:, :, 2 * width :].reshape(groups * piece, width)
    rows_ref[...] = dot(hidden, down_ref[...]).astype(bf16)
    share = gated(got_ref, width)
    for part in range(groups):
        spread_ref[part] = share


def far_down(hidden_ref, down_ref, other_ref, rows_ref):
    own = dot(hidden_ref[...], down_ref[...])
    rows_ref[...] = (own + other_ref[...].astype(f32)).astype(bf16)


def per_device(acts, norm_gain, gate_w, up_w, down_w):
    gate_local, up_local, down_local = gate_w[0, 0], up_w[0, 0], down_w[0, 0]
    tokens, features = acts.shape[1:]
    depth, width = gate_local.shape
    groups_a = features // depth
    near = lax.axis_size("tensor") // 2
    groups_b = near // groups_a
    total = near * tokens
    piece = total // groups_a
    cost = 2 * total * depth * width
    weight = 2 * depth * width

    mirror_acts = flipped(acts[0], near)
    (sent,) = local(
        norm_kernel,
        [(near, tokens, depth)],
        0,
        2 * total * depth,
        acts,
        norm_gain,
        scratch=[
            pltpu.VMEM(acts.shape, bf16),
            pltpu.VMEM(norm_gain.shape, f32),
            pltpu.SemaphoreType.DMA,
            pltpu.SemaphoreType.DMA,
        ],
        fetches=True,
    )
    near_columns = traded(sent, near).reshape(total, depth)
    far_columns = flipped(near_columns, near)

    (sums,) = local(
        gate_up,
        [(total, 2 * width)],
        2 * cost,
        2 * weight,
        near_columns,
        gate_local,
        up_local,
        after=(mirror_acts,),
    )
    shares = traded(sums.reshape(groups_a, piece, 2 * width), groups_a)
    (near_share,) = local(near_share_kernel, [(piece, width)], 0, 2 * total * width, shares)
    (sums,) = local(
        far_sums_near_share,
        [(total, 3 * width)],
        2 * cost,
        2 * weight,
        far_columns,
        near_share,
        gate_local,
        up_local,
    )
    got = traded(sums.reshape(groups_a, piece, 3 * width), groups_a)
    near_rows, spread = local(
        near_down_far_share,
        [(total, depth), (groups_a, piece, width)],
        cost,
        weight,
        got,
        down_local,
    )

    mirror_rows = flipped(near_rows, near)
    hidden = traded(spread, groups_a).reshape(total, width)
    (rows,) = local(far_down, [(total, depth)], cost, weight, hidden, down_local, mirror_rows)
    parts = traded(rows.reshape(near, tokens, depth), near)
    parts = parts.reshape(groups_b, groups_a, tokens, depth).astype(f32)
    summed = jnp.transpose(jnp.sum(parts, axis=0), (1, 0, 2)).reshape(tokens, features)
    block = (mirror_acts.astype(f32) + summed).astype(bf16)
    return passed_along(block[None], near)


def solution(mesh):
    in_specs = (
        P("section", "tensor", None),
        P("section", None),
        P("section", "tensor", None, None),
        P("section", "tensor", None, None),
        P("section", "tensor", None, None),
    )
    out_specs = P("section", "tensor", None)
    return jax.shard_map(
        per_device, mesh=mesh, in_specs=in_specs, out_specs=out_specs, check_vma=False
    )
```

```python
import jax
import jax.numpy as jnp
from jax import lax
from jax.experimental import pallas as pl
from jax.experimental.pallas import tpu as pltpu
from jax.sharding import PartitionSpec as P

f32, bf16 = jnp.float32, jnp.bfloat16


def runs(size):
    count = lax.axis_size("tensor")
    return [list(range(low, low + size)) for low in range(0, count, size)]


def scattered(run, size):
    count = run // size
    places = [(3 * k + 5 * a) % count * size + a for k in range(count) for a in range(size)]
    return [[low + place for place in places] for low in range(0, lax.axis_size("tensor"), run)]


def traded(blocks, groups):
    return lax.all_to_all(blocks, "tensor", 0, 0, axis_index_groups=groups, tiled=True)


def flipped(values, mask):
    count = lax.axis_size("tensor")
    return lax.ppermute(values, "tensor", [(i, i ^ mask) for i in range(count)])


def passed_along(value, mask):
    sections, count = lax.axis_size("section"), lax.axis_size("tensor")
    route = [
        (section * count + place, (section + 1) * count + (place ^ mask))
        for section in range(sections - 1)
        for place in range(count)
    ]
    return lax.ppermute(value, ("section", "tensor"), route)


def dot(left, right):
    return jnp.dot(left, right, preferred_element_type=f32)


def local(body, outs, flops, moved, *operands, after=(), scratch=(), fetches=False):
    spec = pl.BlockSpec(memory_space=pl.ANY if fetches else pltpu.VMEM)
    limit = (56 if fetches else 24) * 2**20

    def kernel(*refs):
        body(*refs[len(after) :])

    return pl.pallas_call(
        kernel,
        out_shape=[jax.ShapeDtypeStruct(shape, bf16) for shape in outs],
        in_specs=[pl.BlockSpec(memory_space=pl.ANY)] * len(after) + [spec] * len(operands),
        out_specs=[pl.BlockSpec(memory_space=pltpu.VMEM)] * len(outs),
        scratch_shapes=scratch,
        compiler_params=pltpu.CompilerParams(vmem_limit_bytes=limit),
        cost_estimate=pl.CostEstimate(flops=flops, bytes_accessed=moved, transcendentals=0),
    )(*after, *operands)


def norm_kernel(acts_hbm, gain_hbm, out_ref, acts_ref, gain_ref, acts_sem, gain_sem):
    acts_copy = pltpu.make_async_copy(acts_hbm, acts_ref, acts_sem)
    gain_copy = pltpu.make_async_copy(gain_hbm, gain_ref, gain_sem)
    acts_copy.start()
    gain_copy.start()
    count, _, depth = out_ref.shape
    acts_copy.wait()
    gain_copy.wait()
    inputs = acts_ref[0].astype(f32)
    groups = inputs.shape[1] // depth
    scale = lax.rsqrt(jnp.mean(inputs * inputs, axis=-1, keepdims=True) + 1e-05)
    normed = (inputs * scale * gain_ref[...]).astype(bf16)
    for block in range(count):
        low = block % groups * depth
        out_ref[block] = normed[:, low : low + depth]


def gate_up(columns_ref, gate_ref, up_ref, out_ref):
    width = gate_ref.shape[1]
    out_ref[:, :width] = dot(columns_ref[...], gate_ref[...]).astype(bf16)
    out_ref[:, width : 2 * width] = dot(columns_ref[...], up_ref[...]).astype(bf16)


def gated(shares_ref, width):
    total = shares_ref[0, :, : 2 * width].astype(f32)
    for part in range(1, shares_ref.shape[0]):
        total = total + shares_ref[part, :, : 2 * width].astype(f32)
    gate = total[:, :width]
    return (gate / (1.0 + jnp.exp(-gate)) * total[:, width:]).astype(bf16)


def near_share_kernel(shares_ref, share_ref):
    share_ref[...] = gated(shares_ref, share_ref.shape[1])


def far_sums_near_share(columns_ref, share_ref, gate_ref, up_ref, out_ref):
    piece, width = share_ref.shape
    gate_up(columns_ref, gate_ref, up_ref, out_ref)
    for low in range(0, out_ref.shape[0], piece):
        out_ref[low : low + piece, 2 * width :] = share_ref[...]


def near_down_far_share(got_ref, down_ref, rows_ref, spread_ref):
    groups, piece, _ = got_ref.shape
    width = down_ref.shape[0]
    hidden = got_ref[:, :, 2 * width :].reshape(groups * piece, width)
    rows_ref[...] = dot(hidden, down_ref[...]).astype(bf16)
    share = gated(got_ref, width)
    for part in range(groups):
        spread_ref[part] = share


def far_down(hidden_ref, down_ref, other_ref, rows_ref):
    own = dot(hidden_ref[...], down_ref[...])
    rows_ref[...] = (own + other_ref[...].astype(f32)).astype(bf16)


def per_device(acts, norm_gain, gate_w, up_w, down_w):
    gate_local, up_local, down_local = gate_w[0, 0], up_w[0, 0], down_w[0, 0]
    tokens, features = acts.shape[1:]
    depth, width = gate_local.shape
    groups_a = features // depth
    near = lax.axis_size("tensor") // 2
    groups_b = near // groups_a
    total = near * tokens
    piece = total // groups_a
    cost = 2 * total * depth * width
    weight = 2 * depth * width
    quads, half = runs(groups_a), scattered(near, groups_a)

    mirror_acts = flipped(acts[0], near)
    (sent,) = local(
        norm_kernel,
        [(near, tokens, depth)],
        0,
        2 * total * depth,
        acts,
        norm_gain,
        scratch=[
            pltpu.VMEM(acts.shape, bf16),
            pltpu.VMEM(norm_gain.shape, f32),
            pltpu.SemaphoreType.DMA,
            pltpu.SemaphoreType.DMA,
        ],
        fetches=True,
    )
    near_columns = traded(sent, half).reshape(total, depth)
    far_columns = flipped(near_columns, near)

    (sums,) = local(
        gate_up,
        [(total, 2 * width)],
        2 * cost,
        2 * weight,
        near_columns,
        gate_local,
        up_local,
        after=(mirror_acts,),
    )
    shares = traded(sums.reshape(groups_a, piece, 2 * width), quads)
    (near_share,) = local(near_share_kernel, [(piece, width)], 0, 2 * total * width, shares)
    (sums,) = local(
        far_sums_near_share,
        [(total, 3 * width)],
        2 * cost,
        2 * weight,
        far_columns,
        near_share,
        gate_local,
        up_local,
    )
    got = traded(sums.reshape(groups_a, piece, 3 * width), quads)
    near_rows, spread = local(
        near_down_far_share,
        [(total, depth), (groups_a, piece, width)],
        cost,
        weight,
        got,
        down_local,
    )

    mirror_rows = flipped(near_rows, near)
    hidden = traded(spread, quads).reshape(total, width)
    (rows,) = local(far_down, [(total, depth)], cost, weight, hidden, down_local, mirror_rows)
    parts = traded(rows.reshape(near, tokens, depth), half)
    parts = parts.reshape(groups_b, groups_a, tokens, depth).astype(f32)
    summed = jnp.transpose(jnp.sum(parts, axis=0), (1, 0, 2)).reshape(tokens, features)
    block = (mirror_acts.astype(f32) + summed).astype(bf16)
    return passed_along(block[None], near)


def solution(mesh):
    in_specs = (
        P("section", "tensor", None),
        P("section", None),
        P("section", "tensor", None, None),
        P("section", "tensor", None, None),
        P("section", "tensor", None, None),
    )
    out_specs = P("section", "tensor", None)
    return jax.shard_map(
        per_device, mesh=mesh, in_specs=in_specs, out_specs=out_specs, check_vma=False
    )
```

```python
import jax
import jax.numpy as jnp
from jax import lax
from jax.experimental import pallas as pl
from jax.experimental.pallas import tpu as pltpu
from jax.sharding import PartitionSpec as P

f32, bf16 = jnp.float32, jnp.bfloat16


def runs(size):
    count = lax.axis_size("tensor")
    return [list(range(low, low + size)) for low in range(0, count, size)]


def scattered(run, size):
    count = run // size
    places = [(3 * k + 5 * a) % count * size + a for k in range(count) for a in range(size)]
    return [[low + place for place in places] for low in range(0, lax.axis_size("tensor"), run)]


def traded(blocks, groups):
    return lax.all_to_all(blocks, "tensor", 0, 0, axis_index_groups=groups, tiled=True)


def flipped(values, mask):
    count = lax.axis_size("tensor")
    return lax.ppermute(values, "tensor", [(i, i ^ mask) for i in range(count)])


def passed_along(value, mask):
    sections, count = lax.axis_size("section"), lax.axis_size("tensor")
    route = [
        (section * count + place, (section + 1) * count + (place ^ mask))
        for section in range(sections - 1)
        for place in range(count)
    ]
    return lax.ppermute(value, ("section", "tensor"), route)


def dot(left, right):
    return jnp.dot(left, right, preferred_element_type=f32)


def local(body, outs, flops, moved, *operands, after=(), scratch=(), fetches=0):
    spec, placed = pl.BlockSpec(memory_space=pltpu.VMEM), pl.BlockSpec(memory_space=pl.ANY)
    limit = (56 if fetches == len(operands) else 24) * 2**20
    left = len(operands) - fetches

    def kernel(*refs):
        body(*refs[len(after) :])

    return pl.pallas_call(
        kernel,
        out_shape=[jax.ShapeDtypeStruct(shape, bf16) for shape in outs],
        in_specs=[placed] * (len(after) + fetches) + [spec] * left,
        out_specs=[spec] * len(outs),
        scratch_shapes=scratch,
        compiler_params=pltpu.CompilerParams(vmem_limit_bytes=limit),
        cost_estimate=pl.CostEstimate(flops=flops, bytes_accessed=moved, transcendentals=0),
    )(*after, *operands)


def norm_kernel(acts_hbm, gain_hbm, out_ref, acts_ref, gain_ref, acts_sem, gain_sem):
    acts_copy = pltpu.make_async_copy(acts_hbm, acts_ref, acts_sem)
    gain_copy = pltpu.make_async_copy(gain_hbm, gain_ref, gain_sem)
    acts_copy.start()
    gain_copy.start()
    count, _, depth = out_ref.shape
    acts_copy.wait()
    gain_copy.wait()
    inputs = acts_ref[0].astype(f32)
    groups = inputs.shape[1] // depth
    scale = lax.rsqrt(jnp.mean(inputs * inputs, axis=-1, keepdims=True) + 1e-05)
    normed = (inputs * scale * gain_ref[...]).astype(bf16)
    for block in range(count):
        low = block % groups * depth
        out_ref[block] = normed[:, low : low + depth]


def gate_up(columns_ref, gate_ref, up_ref, out_ref):
    width = gate_ref.shape[1]
    out_ref[:, :width] = dot(columns_ref[...], gate_ref[...]).astype(bf16)
    out_ref[:, width : 2 * width] = dot(columns_ref[...], up_ref[...]).astype(bf16)


def gated(shares_ref, width):
    total = shares_ref[0, :, : 2 * width].astype(f32)
    for part in range(1, shares_ref.shape[0]):
        total = total + shares_ref[part, :, : 2 * width].astype(f32)
    gate = total[:, :width]
    return (gate / (1.0 + jnp.exp(-gate)) * total[:, width:]).astype(bf16)


def near_share_kernel(shares_ref, share_ref):
    share_ref[...] = gated(shares_ref, share_ref.shape[1])


def far_sums_near_share(far_ref, share_ref, gate_ref, up_ref, out_ref, columns_ref, arrived):
    piece, width = share_ref.shape
    total = out_ref.shape[0]
    halves = [pl.ds(0, total // 2), pl.ds(total // 2, total // 2)]
    fetched = [
        pltpu.make_async_copy(far_ref.at[rows], columns_ref.at[rows], arrived.at[half])
        for half, rows in enumerate(halves)
    ]
    for copy in fetched:
        copy.start()
    for low in range(0, total, piece):
        out_ref[low : low + piece, 2 * width :] = share_ref[...]
    for copy, rows in zip(fetched, halves, strict=True):
        copy.wait()
        gate_up(columns_ref.at[rows], gate_ref, up_ref, out_ref.at[rows])


def near_down_far_share(got_ref, down_ref, rows_ref, spread_ref):
    groups, piece, _ = got_ref.shape
    width = down_ref.shape[0]
    hidden = got_ref[:, :, 2 * width :].reshape(groups * piece, width)
    rows_ref[...] = dot(hidden, down_ref[...]).astype(bf16)
    share = gated(got_ref, width)
    for part in range(groups):
        spread_ref[part] = share


def far_down(hidden_ref, down_ref, other_ref, rows_ref):
    own = dot(hidden_ref[...], down_ref[...])
    rows_ref[...] = (own + other_ref[...].astype(f32)).astype(bf16)


def per_device(acts, norm_gain, gate_w, up_w, down_w):
    gate_local, up_local, down_local = gate_w[0, 0], up_w[0, 0], down_w[0, 0]
    tokens, features = acts.shape[1:]
    depth, width = gate_local.shape
    groups_a = features // depth
    near = lax.axis_size("tensor") // 2
    groups_b = near // groups_a
    total = near * tokens
    piece = total // groups_a
    cost = 2 * total * depth * width
    weight = 2 * depth * width
    quads, half = runs(groups_a), scattered(near, groups_a)

    mirror_acts = flipped(acts[0], near)
    (sent,) = local(
        norm_kernel,
        [(near, tokens, depth)],
        0,
        2 * total * depth,
        acts,
        norm_gain,
        scratch=[
            pltpu.VMEM(acts.shape, bf16),
            pltpu.VMEM(norm_gain.shape, f32),
            pltpu.SemaphoreType.DMA,
            pltpu.SemaphoreType.DMA,
        ],
        fetches=2,
    )
    near_columns = traded(sent, half).reshape(total, depth)
    far_columns = flipped(near_columns, near)

    (sums,) = local(
        gate_up,
        [(total, 2 * width)],
        2 * cost,
        2 * weight,
        near_columns,
        gate_local,
        up_local,
        after=(mirror_acts,),
    )
    shares = traded(sums.reshape(groups_a, piece, 2 * width), quads)
    (near_share,) = local(near_share_kernel, [(piece, width)], 0, 2 * total * width, shares)
    (sums,) = local(
        far_sums_near_share,
        [(total, 3 * width)],
        2 * cost,
        2 * weight,
        far_columns,
        near_share,
        gate_local,
        up_local,
        fetches=1,
        scratch=[pltpu.VMEM((total, depth), bf16), pltpu.SemaphoreType.DMA((2,))],
    )
    got = traded(sums.reshape(groups_a, piece, 3 * width), quads)
    near_rows, spread = local(
        near_down_far_share,
        [(total, depth), (groups_a, piece, width)],
        cost,
        weight,
        got,
        down_local,
    )

    mirror_rows = flipped(near_rows, near)
    hidden = traded(spread, quads).reshape(total, width)
    (rows,) = local(far_down, [(total, depth)], cost, weight, hidden, down_local, mirror_rows)
    parts = traded(rows.reshape(near, tokens, depth), half)
    parts = parts.reshape(groups_b, groups_a, tokens, depth).astype(f32)
    summed = jnp.transpose(jnp.sum(parts, axis=0), (1, 0, 2)).reshape(tokens, features)
    block = (mirror_acts.astype(f32) + summed).astype(bf16)
    return passed_along(block[None], near)


def solution(mesh):
    in_specs = (
        P("section", "tensor", None),
        P("section", None),
        P("section", "tensor", None, None),
        P("section", "tensor", None, None),
        P("section", "tensor", None, None),
    )
    out_specs = P("section", "tensor", None)
    return jax.shard_map(
        per_device, mesh=mesh, in_specs=in_specs, out_specs=out_specs, check_vma=False
    )
```

```python
import jax
import jax.numpy as jnp
from jax import lax
from jax.experimental import pallas as pl
from jax.experimental.pallas import tpu as pltpu
from jax.sharding import PartitionSpec as P

f32, bf16 = jnp.float32, jnp.bfloat16


def runs(size):
    count = lax.axis_size("tensor")
    return [list(range(low, low + size)) for low in range(0, count, size)]


def strided(run, size):
    count = lax.axis_size("tensor")
    return [
        list(range(low + place, low + run, size))
        for low in range(0, count, run)
        for place in range(size)
    ]


def traded(blocks, groups):
    return lax.all_to_all(blocks, "tensor", 0, 0, axis_index_groups=groups, tiled=True)


def flipped(values, mask):
    count = lax.axis_size("tensor")
    return lax.ppermute(values, "tensor", [(i, i ^ mask) for i in range(count)])


def passed_along(value, mask):
    sections, count = lax.axis_size("section"), lax.axis_size("tensor")
    route = [
        (section * count + place, (section + 1) * count + (place ^ mask))
        for section in range(sections - 1)
        for place in range(count)
    ]
    return lax.ppermute(value, ("section", "tensor"), route)


def dot(left, right):
    return jnp.dot(left, right, preferred_element_type=f32)


def local(body, outs, flops, moved, *operands, after=(), scratch=(), fetches=False):
    spec = pl.BlockSpec(memory_space=pl.ANY if fetches else pltpu.VMEM)
    limit = (56 if fetches else 24) * 2**20

    def kernel(*refs):
        body(*refs[len(after) :])

    return pl.pallas_call(
        kernel,
        out_shape=[jax.ShapeDtypeStruct(shape, bf16) for shape in outs],
        in_specs=[pl.BlockSpec(memory_space=pl.ANY)] * len(after) + [spec] * len(operands),
        out_specs=[pl.BlockSpec(memory_space=pltpu.VMEM)] * len(outs),
        scratch_shapes=scratch,
        compiler_params=pltpu.CompilerParams(vmem_limit_bytes=limit),
        cost_estimate=pl.CostEstimate(flops=flops, bytes_accessed=moved, transcendentals=0),
    )(*after, *operands)


def norm_kernel(acts_hbm, gain_hbm, out_ref, acts_ref, gain_ref, acts_sem, gain_sem):
    acts_copy = pltpu.make_async_copy(acts_hbm, acts_ref, acts_sem)
    gain_copy = pltpu.make_async_copy(gain_hbm, gain_ref, gain_sem)
    acts_copy.start()
    gain_copy.start()
    count, _, depth = out_ref.shape
    acts_copy.wait()
    gain_copy.wait()
    inputs = acts_ref[0].astype(f32)
    groups = inputs.shape[1] // depth
    scale = lax.rsqrt(jnp.mean(inputs * inputs, axis=-1, keepdims=True) + 1e-05)
    normed = (inputs * scale * gain_ref[...]).astype(bf16)
    for block in range(count):
        low = block % groups * depth
        out_ref[block] = normed[:, low : low + depth]


def gate_up(columns_ref, gate_ref, up_ref, out_ref):
    width = gate_ref.shape[1]
    out_ref[:, :width] = dot(columns_ref[...], gate_ref[...]).astype(bf16)
    out_ref[:, width : 2 * width] = dot(columns_ref[...], up_ref[...]).astype(bf16)


def gated(shares_ref, width):
    total = shares_ref[0, :, : 2 * width].astype(f32)
    for part in range(1, shares_ref.shape[0]):
        total = total + shares_ref[part, :, : 2 * width].astype(f32)
    gate = total[:, :width]
    return (gate / (1.0 + jnp.exp(-gate)) * total[:, width:]).astype(bf16)


def near_share_kernel(shares_ref, share_ref):
    share_ref[...] = gated(shares_ref, share_ref.shape[1])


def far_sums_near_share(columns_ref, share_ref, gate_ref, up_ref, out_ref):
    piece, width = share_ref.shape
    gate_up(columns_ref, gate_ref, up_ref, out_ref)
    for low in range(0, out_ref.shape[0], piece):
        out_ref[low : low + piece, 2 * width :] = share_ref[...]


def near_down_far_share(got_ref, down_ref, rows_ref, spread_ref):
    groups, piece, _ = got_ref.shape
    width = down_ref.shape[0]
    hidden = got_ref[:, :, 2 * width :].reshape(groups * piece, width)
    rows_ref[...] = dot(hidden, down_ref[...]).astype(bf16)
    share = gated(got_ref, width)
    for part in range(groups):
        spread_ref[part] = share


def far_down(hidden_ref, down_ref, other_ref, rows_ref):
    own = dot(hidden_ref[...], down_ref[...])
    rows_ref[...] = (own + other_ref[...].astype(f32)).astype(bf16)


def per_device(acts, norm_gain, gate_w, up_w, down_w):
    gate_local, up_local, down_local = gate_w[0, 0], up_w[0, 0], down_w[0, 0]
    tokens, features = acts.shape[1:]
    depth, width = gate_local.shape
    groups_a = features // depth
    near = lax.axis_size("tensor") // 2
    total = near * tokens
    piece = total // groups_a
    cost = 2 * total * depth * width
    weight = 2 * depth * width
    quads, line = runs(groups_a), 2 * groups_a

    mirror_acts = flipped(acts[0], near)
    (sent,) = local(
        norm_kernel,
        [(near, tokens, depth)],
        0,
        2 * total * depth,
        acts,
        norm_gain,
        scratch=[
            pltpu.VMEM(acts.shape, bf16),
            pltpu.VMEM(norm_gain.shape, f32),
            pltpu.SemaphoreType.DMA,
            pltpu.SemaphoreType.DMA,
        ],
        fetches=True,
    )
    near_columns = traded(sent, runs(near)).reshape(total, depth)
    far_columns = flipped(near_columns, near)

    (sums,) = local(
        gate_up,
        [(total, 2 * width)],
        2 * cost,
        2 * weight,
        near_columns,
        gate_local,
        up_local,
        after=(mirror_acts,),
    )
    shares = traded(sums.reshape(groups_a, piece, 2 * width), quads)
    (near_share,) = local(near_share_kernel, [(piece, width)], 0, 2 * total * width, shares)
    (sums,) = local(
        far_sums_near_share,
        [(total, 3 * width)],
        2 * cost,
        2 * weight,
        far_columns,
        near_share,
        gate_local,
        up_local,
    )
    got = traded(sums.reshape(groups_a, piece, 3 * width), quads)
    near_rows, spread = local(
        near_down_far_share,
        [(total, depth), (groups_a, piece, width)],
        cost,
        weight,
        got,
        down_local,
    )

    mirror_rows = flipped(near_rows, near)
    hidden = traded(spread, quads).reshape(total, width)
    (rows,) = local(far_down, [(total, depth)], cost, weight, hidden, down_local, mirror_rows)
    parts = traded(rows.reshape(near // line, line * tokens, depth), strided(near, line))
    rows = jnp.sum(parts.astype(f32), axis=0).astype(bf16).reshape(line, tokens, depth)
    parts = traded(rows, runs(line)).reshape(2, groups_a, tokens, depth).astype(f32)
    summed = jnp.transpose(jnp.sum(parts, axis=0), (1, 0, 2)).reshape(tokens, features)
    block = (mirror_acts.astype(f32) + summed).astype(bf16)
    return passed_along(block[None], near)


def solution(mesh):
    in_specs = (
        P("section", "tensor", None),
        P("section", None),
        P("section", "tensor", None, None),
        P("section", "tensor", None, None),
        P("section", "tensor", None, None),
    )
    out_specs = P("section", "tensor", None)
    return jax.shard_map(
        per_device, mesh=mesh, in_specs=in_specs, out_specs=out_specs, check_vma=False
    )
```
